32 devices in a mesh: grp: 2 (over y), orient: 4 (over z), frame: 4 (over x, core).
Axes of the slice: x: 2, y: 2, z: 4, core: 2. Of those that a mesh axis runs over, the one named last changes fastest.
Arguments:
- photons: int32 [1024, 65536], P(('grp', 'frame'), 'orient'), parts along dimension 0, may hold values from 0 to 7
- masses: int32 [1024, 16, 8], P(('grp', 'frame'), 'orient'), parts along dimension 0, may hold values from 1 to 4097, as said below
- maps: int32 [16, 512], P('orient'), may hold values from 0 to 511
- model: float32 [131072], P('grp'), parts along dimension 0, may hold values from 0.2 to 5
- fluence: float32 [1024], P(('grp', 'frame')), parts along dimension 0, may hold values from 0.3 to 3
- level_scale: float32 [8], replicated, may hold values from 0.25 to 4
Outputs:
- gain: float32 [131072], P(('grp', 'orient')), parts along dimension 0
- new_fluence: float32 [1024], P(('grp', 'frame')), parts along dimension 0
The draws below stay inside these ranges and needn't reach their ends.
There are 2 independent parts, one for each index of `grp`. The reference program is written for one: setup_inputs(seed, part) draws one part's arguments, and reference() takes and returns one part's arrays. A program takes and returns all parts, laid end to end along the dimension named above; an argument that names none is the same for every part. Nothing has to cross between parts.
Inputs may be any that keep to these rules, and one draw needn't show every extreme that they name: Positive fixed-point posterior masses.
All inputs are finite; a program needn't handle non-finite values.
Results may differ from the reference program's by a relative error of at most 0.00011.
Values sent between devices are 32-bit elements; how exact they have to be, the bound alone decides.
A program may use at most 64 MiB of HBM per device.

```python
import math
import jax
import jax.numpy as jnp
from jax import lax

PIX = 65536
BLOCK = 128
LEVELS = 8
ITERS = 2
FRAMES = 512
ORIENT = 16


def draw_masses(key, part):
    key = jax.random.fold_in(key, 7)
    key_pop, key_pick, key_level, key_base = jax.random.split(key, 4)
    popular = jnp.left_shift(jnp.ones((ORIENT,), jnp.int32), jax.random.randint(key_pop, (ORIENT,), 0, 5, dtype=jnp.int32))
    cumulative = jnp.cumsum(popular).astype(jnp.int32)
    picks = jax.random.randint(key_pick, (FRAMES,), 0, cumulative[-1], dtype=jnp.int32)
    centre = jnp.sum((cumulative[None, :] <= picks[:, None]).astype(jnp.int32), axis=1)
    level_centre = jax.random.randint(key_level, (FRAMES,), 0, LEVELS, dtype=jnp.int32)
    orient_index = jnp.arange(ORIENT, dtype=jnp.int32)
    level_index = jnp.arange(LEVELS, dtype=jnp.int32)
    offset = jnp.abs(orient_index[None, :] - centre[:, None])
    distance = jnp.minimum(offset, ORIENT - offset)
    level_gap = jnp.abs(level_index[None, :] - level_centre[:, None])
    shifts = jnp.minimum(3 * distance[:, :, None] + level_gap[:, None, :], 30).astype(jnp.int32)
    base_mass = jax.random.randint(key_base, (FRAMES, ORIENT, LEVELS), 2048, 4097, dtype=jnp.int32)
    peak_mask = (distance[:, :, None] == 0) & (level_gap[:, None, :] == 0)
    base_mass = jnp.where(peak_mask, jnp.int32(4096), base_mass)
    return (1 + jnp.right_shift(base_mass, shifts)).astype(jnp.int32)


def touch_ends(result, key, smallest, top_value):
    dims = result.shape
    place = [jax.random.randint(jax.random.fold_in(key, axis), (), 0, dims[axis]) for axis in range(len(dims))]
    result = result.at[tuple(place)].set(smallest)
    longest = dims.index(max(dims))
    place[longest] = (place[longest] + 1) % dims[longest]
    return result.at[tuple(place)].set(top_value)


def levels(key, extent, shards, smallest, top_value):
    level, own = 1.0, jax.random.fold_in(key, 6)
    for dim, parts in shards:
        draws = jnp.exp(jax.random.uniform(jax.random.fold_in(own, dim), (parts,), jnp.float32, smallest / len(shards), top_value / len(shards)))
        level = level * jnp.repeat(draws, extent[dim] // parts).reshape([-1 if axis == dim else 1 for axis in range(len(extent))])
    return level


def setup_inputs(seed: int = 0, part: int = 0) -> dict:
    seeds = jax.random.split(jax.random.key(seed), 7)
    part_splits = jax.random.split(jax.random.fold_in(seeds[6], part), 7)
    return {
        "photons": touch_ends(jax.random.randint(part_splits[0], (FRAMES, PIX), 0, 8), jax.random.fold_in(part_splits[0], 1), 0, 7).astype(jnp.int32),
        "masses": draw_masses(jax.random.fold_in(jax.random.fold_in(seeds[6], part), 71), part),
        "maps": touch_ends(jax.random.randint(seeds[2], (ORIENT, PIX // BLOCK), 0, PIX // BLOCK), jax.random.fold_in(seeds[2], 1), 0, (PIX // BLOCK) - 1).astype(jnp.int32),
        "model": jnp.clip(jnp.exp(jax.random.uniform(part_splits[3], (PIX,), jnp.float32, math.log(0.2), math.log(5.0))), 0.2, 5.0),
        "fluence": jnp.clip(jnp.exp(math.log(3.0) - 2.3025851 * jax.random.uniform(part_splits[4], (FRAMES,), jnp.float32) ** levels(part_splits[4], (FRAMES,), ((0, 4),), -0.2, 0.2)), 0.3, 3.0),
        "level_scale": jnp.clip(jnp.exp(jax.random.uniform(seeds[5], (LEVELS,), jnp.float32, math.log(0.25), math.log(4.0))), 0.25, 4.0),
    }


def reference(photons, masses, maps, model, fluence, level_scale):
    mass = masses.astype(jnp.float32)
    total = jnp.sum(mass, axis=(1, 2))
    prob = mass / total[:, None, None]
    tilted = jnp.sum(prob * level_scale[None, None, :], axis=2)
    frame_photons = jnp.sum(photons, axis=1).astype(jnp.float32)
    pixel_photons = jnp.sum(photons, axis=0).astype(jnp.float32)
    table = model.reshape(PIX // BLOCK, BLOCK)
    slices = table[maps].reshape(maps.shape[0], PIX)
    phi = fluence
    gain = pixel_photons
    for step in range(ITERS):
        weight = jnp.dot(phi, tilted, precision=lax.Precision.HIGHEST)
        expected = jnp.dot(weight, slices, precision=lax.Precision.HIGHEST)
        gain = pixel_photons / expected
        seen = jnp.dot(slices, gain, precision=lax.Precision.HIGHEST)
        phi = frame_photons / jnp.dot(tilted, seen, precision=lax.Precision.HIGHEST)
    return gain, phi
```

```python
import functools
import jax
import jax.numpy as jnp
from jax import lax
from jax.experimental import pallas as pl
from jax.experimental.pallas import tpu as pltpu
from jax.sharding import PartitionSpec as P

BLOCK = 128
ITERS = 2
MESH = pl.DeviceIdType.MESH


def emc_kernel(
    O, F, OL, L, D, MB, NB, CH,
    photons, masses, maps, model, fluence, scale,
    gain_out, phi_out,
    ph, mass_v, flu_v, scale_v, table, map_v, map_s, sl,
    stat, til, cols, parts, note, note_in, gain_v, phi_v,
    ph_sem, in_sem, map_sem, loc_sem, stat_sem, col_sem, note_sem, gain_sem,
):
    N = O * F
    R = O * OL
    o = lax.axis_index("orient")
    f = lax.axis_index("frame")
    me = o * F + f
    width = NB * BLOCK
    piece = width // CH

    def spot(t):
        n = lax.rem(me + t, N)
        return lax.div(n, F), lax.rem(n, F)

    def others(body):
        if N <= 16:
            for t in range(1, N):
                body(t)
        else:
            def step(t, c):
                body(t)
                return c
            lax.fori_loop(1, N, step, 0)

    order = [(F // 2 + i) % F for i in range(F)]
    order = [i for i in order if i != 0] + [0]

    small = [
        pltpu.make_async_copy(masses, mass_v, in_sem.at[0]),
        pltpu.make_async_copy(scale, scale_v, in_sem.at[1]),
        pltpu.make_async_copy(fluence, flu_v, in_sem.at[2]),
        pltpu.make_async_copy(model, table, in_sem.at[3]),
    ]
    first = me * NB
    for c in small:
        c.start()
    own_map = pltpu.make_async_copy(
        maps.at[:, pl.ds(pl.multiple_of(lax.div(first, 128) * 128, 128), 128)], map_v.at[o], in_sem.at[4])
    own_map.start()

    def read(i, c):
        g = lax.rem(f + order[i], F)
        start = pl.multiple_of(g * width + c * piece, 128)
        return pltpu.make_async_copy(
            photons.at[:, pl.ds(start, piece)], ph.at[i, c], ph_sem.at[i, c])

    for i in range(F):
        for c in range(CH):
            read(i, c).start()

    barrier = pltpu.get_barrier_semaphore()

    def greet(t):
        a, b = spot(t)
        pl.semaphore_signal(barrier, inc=1, device_id={"orient": a, "frame": b}, device_id_type=MESH)
    others(greet)

    for c in small[:3]:
        c.wait()
    m = mass_v[...].astype(jnp.float32)
    eye = lax.broadcasted_iota(jnp.int32, (L, L), 0) == lax.broadcasted_iota(jnp.int32, (L, L), 1)
    sc = jnp.sum(jnp.where(eye, jnp.broadcast_to(scale_v[...], (L, L)), 0.0), axis=1, keepdims=True)
    tot = jnp.zeros((1, D), jnp.float32)
    for k in range(OL):
        stat[me, k:k + 1, :] = jnp.sum(m[k] * sc, axis=0, keepdims=True)
        tot += jnp.sum(m[k], axis=0, keepdims=True)
    stat[me, OL:OL + 1, :] = tot
    stat[me, OL + 1:OL + 2, :] = flu_v[...]

    pl.semaphore_wait(barrier, N - 1)

    def send_map(t):
        a = lax.rem(o + t, O)
        block = lax.div((a * F + f) * NB, 128)
        return pltpu.make_async_remote_copy(
            src_ref=maps.at[:, pl.ds(pl.multiple_of(block * 128, 128), 128)],
            dst_ref=map_v.at[o], send_sem=map_sem.at[0], recv_sem=map_sem.at[1],
            device_id={"orient": a}, device_id_type=MESH)
    for t in range(1, O):
        send_map(t).start()

    def send_stat(t):
        a, b = spot(t)
        pltpu.make_async_remote_copy(
            src_ref=stat.at[me], dst_ref=stat.at[me], send_sem=stat_sem.at[0], recv_sem=stat_sem.at[1],
            device_id={"orient": a, "frame": b}, device_id_type=MESH).start()
    others(send_stat)

    def sums(i, rows):
        for c in range(CH):
            read(i, c).wait()

            def tile(q, acc):
                x = ph[i, c, :, pl.ds(pl.multiple_of(q * 128, 128), 128)]
                cols[i, pl.ds(c * (piece // 128) + q, 1), :] = jnp.sum(x, axis=0, keepdims=True).astype(jnp.float32)
                return acc + x
            rows = lax.fori_loop(0, piece // 128, tile, rows, unroll=2)
        return rows

    def send_cols(i):
        pltpu.make_async_remote_copy(
            src_ref=cols.at[i], dst_ref=parts.at[f], send_sem=col_sem.at[0], recv_sem=col_sem.at[1],
            device_id={"frame": lax.rem(f + order[i], F)}, device_id_type=MESH).start()

    def all_of(ref, sem, count):
        c = pltpu.make_async_remote_copy(
            src_ref=ref.at[pl.ds(0, count)], dst_ref=ref.at[pl.ds(0, count)],
            send_sem=sem.at[0], recv_sem=sem.at[1],
            device_id={"orient": lax.rem(o + 1, O)}, device_id_type=MESH)
        return c

    rows = jnp.zeros((D, 128), jnp.int32)
    half = F // 2
    for i in range(half):
        rows = sums(i, rows)
        send_cols(i)

    own_map.wait()
    maps_in = all_of(map_v, map_sem, O - 1)
    maps_in.wait_recv()
    to_s = pltpu.make_async_copy(map_v, map_s, loc_sem.at[0])
    to_s.start()
    small[3].wait()

    stats_in = all_of(stat, stat_sem, N - 1)
    stats_in.wait_recv()
    for g in range(F):
        t = stat[g, OL:OL + 1, :]
        for a in range(1, O):
            t += stat[a * F + g, OL:OL + 1, :]
        inv = 1.0 / t
        for a in range(O):
            til[g, a * OL:(a + 1) * OL, :] = stat[a * F + g, 0:OL, :] * inv

    to_s.wait()
    base = lax.rem(first, 128)

    def look(r, carry):
        a, k = lax.div(r, OL), lax.rem(r, OL)
        for b in range(NB):
            sl[r, b:b + 1, :] = table[pl.ds(map_s[a, k, base + b], 1), :]
        return carry
    lax.fori_loop(0, R, look, 0)

    def expected_of(phis):
        w = til[0] * phis[0]
        for g in range(1, F):
            w += til[g] * phis[g]
        w = jnp.broadcast_to(jnp.sum(w, axis=1, keepdims=True), (R, BLOCK))
        e = sl[0] * w[0:1, :]
        for r in range(1, R):
            e += sl[r] * w[r:r + 1, :]
        return e

    expected = expected_of([stat[g, OL + 1:OL + 2, :] for g in range(F)])

    for i in range(half, F):
        rows = sums(i, rows)
        if i < F - 1:
            send_cols(i)

    note[0, 1:2, :] = jnp.sum(rows.astype(jnp.float32).T, axis=0, keepdims=True)
    parts[f] = cols[F - 1]
    parts_in = all_of(parts, col_sem, F - 1)
    parts_in.wait_recv()
    pixel = parts[0]
    for g in range(1, F):
        pixel += parts[g]

    diag = lax.broadcasted_iota(jnp.int32, (R, 128), 0) == lax.broadcasted_iota(jnp.int32, (R, 128), 1)

    for step in range(ITERS):
        gain = pixel / expected
        if step == ITERS - 1:
            gain_v[f] = gain

            for t in range(1, F):
                pltpu.make_async_remote_copy(
                    src_ref=gain_v.at[f], dst_ref=gain_v.at[f], send_sem=gain_sem.at[0], recv_sem=gain_sem.at[1],
                    device_id={"frame": lax.rem(f + t, F)}, device_id_type=MESH).start()
        part = [jnp.sum(sl[r] * gain, axis=0, keepdims=True) for r in range(R)]
        part = jnp.sum(jnp.concatenate(part, axis=0), axis=1, keepdims=True)
        row = jnp.sum(jnp.where(diag, part, 0.0), axis=0, keepdims=True)
        note[step, 0:1, :] = row
        if step > 0:
            note[step, 1:2, :] = jnp.zeros((1, 128), jnp.float32)
        note_in[step, me] = note[step]

        def send_note(t):
            a, b = spot(t)
            pltpu.make_async_remote_copy(
                src_ref=note.at[step], dst_ref=note_in.at[step, me],
                send_sem=note_sem.at[step, 0], recv_sem=note_sem.at[step, 1],
                device_id={"orient": a, "frame": b}, device_id_type=MESH).start()
        others(send_note)
        notes = all_of(note_in.at[step], note_sem.at[step], N - 1)
        notes.wait_recv()
        seen = note_in[step, 0, 0:1, :]
        for n in range(1, N):
            seen += note_in[step, n, 0:1, :]
        seen = jnp.sum(jnp.where(diag, seen, 0.0), axis=1, keepdims=True)

        def photons_of(g):
            t = note_in[0, g, 1:2, :]
            for a in range(1, O):
                t += note_in[0, a * F + g, 1:2, :]
            return t
        if step < ITERS - 1:
            phis = [photons_of(g) / jnp.sum(til[g] * seen, axis=0, keepdims=True) for g in range(F)]
            expected = expected_of(phis)
        else:
            phi_v[...] = photons_of(f) / jnp.sum(til[f] * seen, axis=0, keepdims=True)
        notes.wait_send()

    phi_write = pltpu.make_async_copy(phi_v, phi_out, loc_sem.at[1])
    phi_write.start()
    gains = all_of(gain_v, gain_sem, F - 1)
    gains.wait_recv()
    gain_write = pltpu.make_async_copy(gain_v, gain_out, loc_sem.at[2])
    gain_write.start()
    maps_in.wait_send()
    stats_in.wait_send()
    parts_in.wait_send()
    gains.wait_send()
    phi_write.wait()
    gain_write.wait()


def on_device(O, F, photons, masses, maps, model, fluence, level_scale):
    D, OL, L = masses.shape
    wide = photons.shape[1]
    MB = maps.shape[1]
    N = O * F
    NB = wide // F // BLOCK
    CH = 2 if NB % 2 == 0 else 1
    R = O * OL
    f32, i32 = jnp.float32, jnp.int32
    V = pltpu.VMEM
    dma = pltpu.SemaphoreType.DMA
    SR = -(-(OL + 2) // 8) * 8
    body = functools.partial(emc_kernel, O, F, OL, L, D, MB, NB, CH)
    hbm = pl.BlockSpec(memory_space=pltpu.HBM)
    gain, phi = pl.pallas_call(
        body,
        out_shape=(jax.ShapeDtypeStruct((F, NB, BLOCK), f32), jax.ShapeDtypeStruct((1, D), f32)),
        in_specs=[hbm] * 6,
        out_specs=(hbm, hbm),
        scratch_shapes=[
            V((F, CH, D, NB * BLOCK // CH), i32),
            V((OL, L, D), i32), V((1, D), f32), V((1, L), f32),
            V((MB, BLOCK), f32), V((O, OL, 128), i32), pltpu.SMEM((O, OL, 128), i32),
            V((R, NB, BLOCK), f32), V((N, SR, D), f32), V((F, R, D), f32),
            V((F, NB, BLOCK), f32), V((F, NB, BLOCK), f32),
            V((ITERS, 2, 128), f32), V((ITERS, N, 2, 128), f32),
            V((F, NB, BLOCK), f32), V((1, D), f32),
            dma((F, CH)), dma((5,)), dma((2,)), dma((3,)), dma((2,)), dma((2,)), dma((ITERS, 2)), dma((2,)),
        ],
        compiler_params=pltpu.CompilerParams(
            collective_id=0, has_side_effects=True, vmem_limit_bytes=40 * 1024 * 1024),
    )(photons, jnp.transpose(masses, (1, 2, 0)), maps, model.reshape(MB, BLOCK),
      fluence.reshape(1, D), level_scale.reshape(1, L))
    return gain.reshape(-1), phi.reshape(-1)


def solution(mesh):
    placed = (
        P(("grp", "frame"), "orient"),
        P(("grp", "frame"), "orient", None),
        P("orient", None),
        P("grp"),
        P(("grp", "frame")),
        P(),
    )
    O, F = mesh.shape["orient"], mesh.shape["frame"]

    def run(*args):
        return on_device(O, F, *args)

    return jax.shard_map(
        run,
        mesh=mesh,
        in_specs=placed,
        out_specs=(P(("grp", "orient")), P(("grp", "frame"))),
        check_vma=False,
    )
```

```python
import functools
import jax
import jax.numpy as jnp
from jax import lax
from jax.experimental import pallas as pl
from jax.experimental.pallas import tpu as pltpu
from jax.sharding import PartitionSpec as P

BLOCK = 128
ITERS = 2
MESH = pl.DeviceIdType.MESH


def emc_kernel(
    O, F, OL, L, D, MB, NB, CH,
    photons, masses, maps, model, fluence, scale,
    gain_out, phi_out,
    ph, mass_v, flu_v, scale_v, table, map_v, map_s, sl,
    stat, til, cols, parts, note, note_in, gain_v, phi_v,
    ph_sem, in_sem, map_sem, loc_sem, stat_sem, col_sem, note_sem, gain_sem,
):
    N = O * F
    R = O * OL
    o = lax.axis_index("orient")
    f = lax.axis_index("frame")
    me = o * F + f
    width = NB * BLOCK
    piece = width // CH

    def spot(t):
        n = lax.rem(me + t, N)
        return lax.div(n, F), lax.rem(n, F)

    def others(body):
        if N <= 16:
            for t in range(1, N):
                body(t)
        else:
            def step(t, c):
                body(t)
                return c
            lax.fori_loop(1, N, step, 0)

    order = [(F // 2 + i) % F for i in range(F)]
    order = [i for i in order if i != 0] + [0]

    small = [
        pltpu.make_async_copy(masses, mass_v, in_sem.at[0]),
        pltpu.make_async_copy(scale, scale_v, in_sem.at[1]),
        pltpu.make_async_copy(fluence, flu_v, in_sem.at[2]),
        pltpu.make_async_copy(model, table, in_sem.at[3]),
    ]
    first = me * NB
    for c in small:
        c.start()
    own_map = pltpu.make_async_copy(
        maps.at[:, pl.ds(pl.multiple_of(lax.div(first, 128) * 128, 128), 128)], map_v.at[o], in_sem.at[4])
    own_map.start()

    def read(i, c):
        g = lax.rem(f + order[i], F)
        start = pl.multiple_of(g * width + c * piece, 128)
        return pltpu.make_async_copy(
            photons.at[:, pl.ds(start, piece)], ph.at[i, c], ph_sem.at[i, c])

    for i in range(F):
        for c in range(CH):
            read(i, c).start()

    barrier = pltpu.get_barrier_semaphore()

    def greet(t):
        a, b = spot(t)
        pl.semaphore_signal(barrier, inc=1, device_id={"orient": a, "frame": b}, device_id_type=MESH)
    others(greet)

    for c in small[:3]:
        c.wait()
    m = mass_v[...].astype(jnp.float32)
    eye = lax.broadcasted_iota(jnp.int32, (L, L), 0) == lax.broadcasted_iota(jnp.int32, (L, L), 1)
    sc = jnp.sum(jnp.where(eye, jnp.broadcast_to(scale_v[...], (L, L)), 0.0), axis=1, keepdims=True)
    tot = jnp.zeros((1, D), jnp.float32)
    for k in range(OL):
        stat[me, k:k + 1, :] = jnp.sum(m[k] * sc, axis=0, keepdims=True)
        tot += jnp.sum(m[k], axis=0, keepdims=True)
    stat[me, OL:OL + 1, :] = tot
    stat[me, OL + 1:OL + 2, :] = flu_v[...]

    pl.semaphore_wait(barrier, N - 1)

    def send_map(t):
        a = lax.rem(o + t, O)
        block = lax.div((a * F + f) * NB, 128)
        return pltpu.make_async_remote_copy(
            src_ref=maps.at[:, pl.ds(pl.multiple_of(block * 128, 128), 128)],
            dst_ref=map_v.at[o], send_sem=map_sem.at[0], recv_sem=map_sem.at[1],
            device_id={"orient": a}, device_id_type=MESH)
    for t in range(1, O):
        send_map(t).start()

    def send_stat(t):
        a, b = spot(t)
        pltpu.make_async_remote_copy(
            src_ref=stat.at[me], dst_ref=stat.at[me], send_sem=stat_sem.at[0], recv_sem=stat_sem.at[1],
            device_id={"orient": a, "frame": b}, device_id_type=MESH).start()
    others(send_stat)

    def sums(i, rows):
        for c in range(CH):
            read(i, c).wait()

            def tile(q, acc):
                x = ph[i, c, :, pl.ds(pl.multiple_of(q * 128, 128), 128)]
                cols[i, pl.ds(c * (piece // 128) + q, 1), :] = jnp.sum(x, axis=0, keepdims=True).astype(jnp.float32)
                return acc + x
            rows = lax.fori_loop(0, piece // 128, tile, rows, unroll=2)
        return rows

    def send_cols(i):
        pltpu.make_async_remote_copy(
            src_ref=cols.at[i], dst_ref=parts.at[f], send_sem=col_sem.at[0], recv_sem=col_sem.at[1],
            device_id={"frame": lax.rem(f + order[i], F)}, device_id_type=MESH).start()

    def all_of(ref, sem, count):
        c = pltpu.make_async_remote_copy(
            src_ref=ref.at[pl.ds(0, count)], dst_ref=ref.at[pl.ds(0, count)],
            send_sem=sem.at[0], recv_sem=sem.at[1],
            device_id={"orient": lax.rem(o + 1, O)}, device_id_type=MESH)
        return c

    rows = jnp.zeros((D, 128), jnp.int32)
    for i in range(F):
        rows = sums(i, rows)
        if i < F - 1:
            send_cols(i)

    note[0, 1:2, :] = jnp.sum(rows.astype(jnp.float32).T, axis=0, keepdims=True)
    parts[f] = cols[F - 1]

    own_map.wait()
    maps_in = all_of(map_v, map_sem, O - 1)
    maps_in.wait_recv()
    to_s = pltpu.make_async_copy(map_v, map_s, loc_sem.at[0])
    to_s.start()
    small[3].wait()

    stats_in = all_of(stat, stat_sem, N - 1)
    stats_in.wait_recv()
    for g in range(F):
        t = stat[g, OL:OL + 1, :]
        for a in range(1, O):
            t += stat[a * F + g, OL:OL + 1, :]
        inv = 1.0 / t
        for a in range(O):
            til[g, a * OL:(a + 1) * OL, :] = stat[a * F + g, 0:OL, :] * inv

    to_s.wait()
    base = lax.rem(first, 128)

    def look(r, carry):
        a, k = lax.div(r, OL), lax.rem(r, OL)
        for b in range(NB):
            sl[r, b:b + 1, :] = table[pl.ds(map_s[a, k, base + b], 1), :]
        return carry
    lax.fori_loop(0, R, look, 0)

    def expected_of(phis):
        w = til[0] * phis[0]
        for g in range(1, F):
            w += til[g] * phis[g]
        w = jnp.broadcast_to(jnp.sum(w, axis=1, keepdims=True), (R, BLOCK))
        e = sl[0] * w[0:1, :]
        for r in range(1, R):
            e += sl[r] * w[r:r + 1, :]
        return e

    expected = expected_of([stat[g, OL + 1:OL + 2, :] for g in range(F)])

    parts_in = all_of(parts, col_sem, F - 1)
    parts_in.wait_recv()
    pixel = parts[0]
    for g in range(1, F):
        pixel += parts[g]

    diag = lax.broadcasted_iota(jnp.int32, (R, 128), 0) == lax.broadcasted_iota(jnp.int32, (R, 128), 1)

    for step in range(ITERS):
        gain = pixel / expected
        if step == ITERS - 1:
            gain_v[f] = gain

            for t in range(1, F):
                pltpu.make_async_remote_copy(
                    src_ref=gain_v.at[f], dst_ref=gain_v.at[f], send_sem=gain_sem.at[0], recv_sem=gain_sem.at[1],
                    device_id={"frame": lax.rem(f + t, F)}, device_id_type=MESH).start()
        part = [jnp.sum(sl[r] * gain, axis=0, keepdims=True) for r in range(R)]
        part = jnp.sum(jnp.concatenate(part, axis=0), axis=1, keepdims=True)
        row = jnp.sum(jnp.where(diag, part, 0.0), axis=0, keepdims=True)
        note[step, 0:1, :] = row
        if step > 0:
            note[step, 1:2, :] = jnp.zeros((1, 128), jnp.float32)
        note_in[step, me] = note[step]

        def send_note(t):
            a, b = spot(t)
            pltpu.make_async_remote_copy(
                src_ref=note.at[step], dst_ref=note_in.at[step, me],
                send_sem=note_sem.at[step, 0], recv_sem=note_sem.at[step, 1],
                device_id={"orient": a, "frame": b}, device_id_type=MESH).start()
        others(send_note)
        notes = all_of(note_in.at[step], note_sem.at[step], N - 1)
        notes.wait_recv()
        seen = note_in[step, 0, 0:1, :]
        for n in range(1, N):
            seen += note_in[step, n, 0:1, :]
        seen = jnp.sum(jnp.where(diag, seen, 0.0), axis=1, keepdims=True)

        def photons_of(g):
            t = note_in[0, g, 1:2, :]
            for a in range(1, O):
                t += note_in[0, a * F + g, 1:2, :]
            return t
        if step < ITERS - 1:
            phis = [photons_of(g) / jnp.sum(til[g] * seen, axis=0, keepdims=True) for g in range(F)]
            expected = expected_of(phis)
        else:
            phi_v[...] = photons_of(f) / jnp.sum(til[f] * seen, axis=0, keepdims=True)
        notes.wait_send()

    phi_write = pltpu.make_async_copy(phi_v, phi_out, loc_sem.at[1])
    phi_write.start()
    gains = all_of(gain_v, gain_sem, F - 1)
    gains.wait_recv()
    gain_write = pltpu.make_async_copy(gain_v, gain_out, loc_sem.at[2])
    gain_write.start()
    maps_in.wait_send()
    stats_in.wait_send()
    parts_in.wait_send()
    gains.wait_send()
    phi_write.wait()
    gain_write.wait()


def on_device(O, F, photons, masses, maps, model, fluence, level_scale):
    D, OL, L = masses.shape
    wide = photons.shape[1]
    MB = maps.shape[1]
    N = O * F
    NB = wide // F // BLOCK
    CH = 2 if NB % 2 == 0 else 1
    R = O * OL
    f32, i32 = jnp.float32, jnp.int32
    V = pltpu.VMEM
    dma = pltpu.SemaphoreType.DMA
    SR = -(-(OL + 2) // 8) * 8
    body = functools.partial(emc_kernel, O, F, OL, L, D, MB, NB, CH)
    hbm = pl.BlockSpec(memory_space=pltpu.HBM)
    gain, phi = pl.pallas_call(
        body,
        out_shape=(pltpu.VMEM((F, NB, BLOCK), f32), pltpu.VMEM((1, D), f32)),
        in_specs=[hbm] * 6,
        out_specs=(pl.BlockSpec(memory_space=pltpu.VMEM),)*2,
        scratch_shapes=[
            V((F, CH, D, NB * BLOCK // CH), i32),
            V((OL, L, D), i32), V((1, D), f32), V((1, L), f32),
            V((MB, BLOCK), f32), V((O, OL, 128), i32), pltpu.SMEM((O, OL, 128), i32),
            V((R, NB, BLOCK), f32), V((N, SR, D), f32), V((F, R, D), f32),
            V((F, NB, BLOCK), f32), V((F, NB, BLOCK), f32),
            V((ITERS, 2, 128), f32), V((ITERS, N, 2, 128), f32),
            V((F, NB, BLOCK), f32), V((1, D), f32),
            dma((F, CH)), dma((5,)), dma((2,)), dma((3,)), dma((2,)), dma((2,)), dma((ITERS, 2)), dma((2,)),
        ],
        compiler_params=pltpu.CompilerParams(
            collective_id=0, has_side_effects=True, vmem_limit_bytes=63 * 1024 * 1024),
    )(photons, jnp.transpose(masses, (1, 2, 0)), maps, model.reshape(MB, BLOCK),
      fluence.reshape(1, D), level_scale.reshape(1, L))
    return gain.reshape(-1), phi.reshape(-1)


def solution(mesh):
    placed = (
        P(("grp", "frame"), "orient"),
        P(("grp", "frame"), "orient", None),
        P("orient", None),
        P("grp"),
        P(("grp", "frame")),
        P(),
    )
    O, F = mesh.shape["orient"], mesh.shape["frame"]

    def run(*args):
        return on_device(O, F, *args)

    return jax.shard_map(
        run,
        mesh=mesh,
        in_specs=placed,
        out_specs=(P(("grp", "orient")), P(("grp", "frame"))),
        check_vma=False,
    )
```

```python
import functools
import jax
import jax.numpy as jnp
from jax import lax
from jax.experimental import pallas as pl
from jax.experimental.pallas import tpu as pltpu
from jax.sharding import PartitionSpec as P

BLOCK = 128
ITERS = 2
MESH = pl.DeviceIdType.MESH


def emc_kernel(
    O, F, OL, L, D, MB, NB, CH,
    photons, masses, maps, model, fluence, scale,
    gain_out, phi_out,
    ph, mass_v, flu_v, scale_v, table, map_v, map_s, sl,
    stat, til, cols, parts, note, note_in, gain_v, phi_v,
    ph_sem, in_sem, map_sem, loc_sem, stat_sem, col_sem, note_sem, gain_sem,
):
    N = O * F
    R = O * OL
    o = lax.axis_index("orient")
    f = lax.axis_index("frame")
    me = o * F + f
    width = NB * BLOCK
    piece = width // CH
    U = 8 if piece % 1024 == 0 else 1

    def spot(t):
        n = lax.rem(me + t, N)
        return lax.div(n, F), lax.rem(n, F)

    def others(body):
        if N <= 16:
            for t in range(1, N):
                body(t)
        else:
            def step(t, c):
                body(t)
                return c
            lax.fori_loop(1, N, step, 0)

    order = [(F // 2 + i) % F for i in range(F)]
    order = [i for i in order if i != 0] + [0]

    small = [
        pltpu.make_async_copy(masses, mass_v, in_sem.at[0]),
        pltpu.make_async_copy(scale, scale_v, in_sem.at[1]),
        pltpu.make_async_copy(fluence, flu_v, in_sem.at[2]),
        pltpu.make_async_copy(model, table, in_sem.at[3]),
    ]
    first = me * NB
    for c in small:
        c.start()
    own_map = pltpu.make_async_copy(
        maps.at[:, pl.ds(pl.multiple_of(lax.div(first, 128) * 128, 128), 128)], map_v.at[o], in_sem.at[4])
    own_map.start()

    def read(i, c):
        g = lax.rem(f + order[i], F)
        start = pl.multiple_of(g * width + c * piece, 128)
        return pltpu.make_async_copy(
            photons.at[:, pl.ds(start, piece)], ph.at[i, c], ph_sem.at[i, c])

    for i in range(F):
        for c in range(CH):
            read(i, c).start()

    barrier = pltpu.get_barrier_semaphore()

    def greet(t):
        a, b = spot(t)
        pl.semaphore_signal(barrier, inc=1, device_id={"orient": a, "frame": b}, device_id_type=MESH)
    others(greet)

    for c in small[:3]:
        c.wait()
    m = mass_v[...].astype(jnp.float32)
    eye = lax.broadcasted_iota(jnp.int32, (L, L), 0) == lax.broadcasted_iota(jnp.int32, (L, L), 1)
    sc = jnp.sum(jnp.where(eye, jnp.broadcast_to(scale_v[...], (L, L)), 0.0), axis=1, keepdims=True)
    tot = jnp.zeros((1, D), jnp.float32)
    for k in range(OL):
        stat[me, k:k + 1, :] = jnp.sum(m[k] * sc, axis=0, keepdims=True)
        tot += jnp.sum(m[k], axis=0, keepdims=True)
    stat[me, OL:OL + 1, :] = tot
    stat[me, OL + 1:OL + 2, :] = flu_v[...]

    pl.semaphore_wait(barrier, N - 1)

    def send_map(t):
        a = lax.rem(o + t, O)
        block = lax.div((a * F + f) * NB, 128)
        return pltpu.make_async_remote_copy(
            src_ref=maps.at[:, pl.ds(pl.multiple_of(block * 128, 128), 128)],
            dst_ref=map_v.at[o], send_sem=map_sem.at[0], recv_sem=map_sem.at[1],
            device_id={"orient": a}, device_id_type=MESH)
    for t in range(1, O):
        send_map(t).start()

    def send_stat(t):
        a, b = spot(t)
        pltpu.make_async_remote_copy(
            src_ref=stat.at[me], dst_ref=stat.at[me], send_sem=stat_sem.at[0], recv_sem=stat_sem.at[1],
            device_id={"orient": a, "frame": b}, device_id_type=MESH).start()
    others(send_stat)

    def sums(i, rows):
        for c in range(CH):
            read(i, c).wait()

            def tiles(q, acc):
                out = []
                for u in range(U):
                    x = ph[i, c, :, pl.ds(pl.multiple_of((q * U + u) * 128, 128), 128)].reshape(D // 8, 8, 128)
                    col = x[0]
                    for d in range(1, D // 8):
                        col += x[d]
                    out.append(jnp.sum(col, axis=0, keepdims=True))
                    acc += x.reshape(D, 128)
                here = pl.multiple_of(c * (piece // 128) + q * U, U)
                cols[i, pl.ds(here, U), :] = jnp.concatenate(out, axis=0).astype(jnp.float32)
                return acc
            rows = lax.fori_loop(0, piece // 128 // U, tiles, rows)
        return rows

    def send_cols(i):
        pltpu.make_async_remote_copy(
            src_ref=cols.at[i], dst_ref=parts.at[f], send_sem=col_sem.at[0], recv_sem=col_sem.at[1],
            device_id={"frame": lax.rem(f + order[i], F)}, device_id_type=MESH).start()

    def all_of(ref, sem, count):
        c = pltpu.make_async_remote_copy(
            src_ref=ref.at[pl.ds(0, count)], dst_ref=ref.at[pl.ds(0, count)],
            send_sem=sem.at[0], recv_sem=sem.at[1],
            device_id={"orient": lax.rem(o + 1, O)}, device_id_type=MESH)
        return c

    rows = jnp.zeros((D, 128), jnp.int32)
    for i in range(F):
        rows = sums(i, rows)
        if i < F - 1:
            send_cols(i)

    note[0, 1:2, :] = jnp.sum(rows.astype(jnp.float32).T, axis=0, keepdims=True)
    parts[f] = cols[F - 1]

    own_map.wait()
    maps_in = all_of(map_v, map_sem, O - 1)
    maps_in.wait_recv()
    to_s = pltpu.make_async_copy(map_v, map_s, loc_sem.at[0])
    to_s.start()
    small[3].wait()

    stats_in = all_of(stat, stat_sem, N - 1)
    stats_in.wait_recv()
    for g in range(F):
        t = stat[g, OL:OL + 1, :]
        for a in range(1, O):
            t += stat[a * F + g, OL:OL + 1, :]
        inv = 1.0 / t
        for a in range(O):
            til[g, a * OL:(a + 1) * OL, :] = stat[a * F + g, 0:OL, :] * inv

    to_s.wait()
    base = lax.rem(first, 128)

    def look(r, carry):
        a, k = lax.div(r, OL), lax.rem(r, OL)
        got = [table[pl.ds(map_s[a, k, base + b], 1), :] for b in range(NB)]
        for b in range(NB):
            sl[r, b:b + 1, :] = got[b]
        return carry
    lax.fori_loop(0, R, look, 0)

    def expected_of(phis):
        w = til[0] * phis[0]
        for g in range(1, F):
            w += til[g] * phis[g]
        w = jnp.broadcast_to(jnp.sum(w, axis=1, keepdims=True), (R, BLOCK))
        e = sl[0] * w[0:1, :]
        for r in range(1, R):
            e += sl[r] * w[r:r + 1, :]
        return e

    expected = expected_of([stat[g, OL + 1:OL + 2, :] for g in range(F)])

    parts_in = all_of(parts, col_sem, F - 1)
    parts_in.wait_recv()
    pixel = parts[0]
    for g in range(1, F):
        pixel += parts[g]

    diag = lax.broadcasted_iota(jnp.int32, (R, 128), 0) == lax.broadcasted_iota(jnp.int32, (R, 128), 1)

    for step in range(ITERS):
        gain = pixel / expected
        if step == ITERS - 1:
            gain_v[f] = gain

            for t in range(1, F):
                pltpu.make_async_remote_copy(
                    src_ref=gain_v.at[f], dst_ref=gain_v.at[f], send_sem=gain_sem.at[0], recv_sem=gain_sem.at[1],
                    device_id={"frame": lax.rem(f + t, F)}, device_id_type=MESH).start()
        part = [jnp.sum(sl[r] * gain, axis=0, keepdims=True) for r in range(R)]
        part = jnp.sum(jnp.concatenate(part, axis=0), axis=1, keepdims=True)
        row = jnp.sum(jnp.where(diag, part, 0.0), axis=0, keepdims=True)
        note[step, 0:1, :] = row
        if step > 0:
            note[step, 1:2, :] = jnp.zeros((1, 128), jnp.float32)
        note_in[step, me] = note[step]

        def send_note(t):
            a, b = spot(t)
            pltpu.make_async_remote_copy(
                src_ref=note.at[step], dst_ref=note_in.at[step, me],
                send_sem=note_sem.at[step, 0], recv_sem=note_sem.at[step, 1],
                device_id={"orient": a, "frame": b}, device_id_type=MESH).start()
        others(send_note)
        notes = all_of(note_in.at[step], note_sem.at[step], N - 1)
        notes.wait_recv()
        seen = note_in[step, 0, 0:1, :]
        for n in range(1, N):
            seen += note_in[step, n, 0:1, :]
        seen = jnp.sum(jnp.where(diag, seen, 0.0), axis=1, keepdims=True)

        def photons_of(g):
            t = note_in[0, g, 1:2, :]
            for a in range(1, O):
                t += note_in[0, a * F + g, 1:2, :]
            return t
        if step < ITERS - 1:
            phis = [photons_of(g) / jnp.sum(til[g] * seen, axis=0, keepdims=True) for g in range(F)]
            expected = expected_of(phis)
        else:
            phi_v[...] = photons_of(f) / jnp.sum(til[f] * seen, axis=0, keepdims=True)
        notes.wait_send()

    phi_write = pltpu.make_async_copy(phi_v, phi_out, loc_sem.at[1])
    phi_write.start()
    gains = all_of(gain_v, gain_sem, F - 1)
    gains.wait_recv()
    gain_write = pltpu.make_async_copy(gain_v, gain_out, loc_sem.at[2])
    gain_write.start()
    maps_in.wait_send()
    stats_in.wait_send()
    parts_in.wait_send()
    gains.wait_send()
    phi_write.wait()
    gain_write.wait()


def on_device(O, F, photons, masses, maps, model, fluence, level_scale):
    D, OL, L = masses.shape
    wide = photons.shape[1]
    MB = maps.shape[1]
    N = O * F
    NB = wide // F // BLOCK
    CH = 1
    R = O * OL
    f32, i32 = jnp.float32, jnp.int32
    V = pltpu.VMEM
    dma = pltpu.SemaphoreType.DMA
    SR = -(-(OL + 2) // 8) * 8
    body = functools.partial(emc_kernel, O, F, OL, L, D, MB, NB, CH)
    hbm = pl.BlockSpec(memory_space=pltpu.HBM)
    gain, phi = pl.pallas_call(
        body,
        out_shape=(pltpu.VMEM((F, NB, BLOCK), f32), pltpu.VMEM((1, D), f32)),
        in_specs=[hbm] * 6,
        out_specs=(pl.BlockSpec(memory_space=pltpu.VMEM),)*2,
        scratch_shapes=[
            V((F, CH, D, NB * BLOCK // CH), i32),
            V((OL, L, D), i32), V((1, D), f32), V((1, L), f32),
            V((MB, BLOCK), f32), V((O, OL, 128), i32), pltpu.SMEM((O, OL, 128), i32),
            V((R, NB, BLOCK), f32), V((N, SR, D), f32), V((F, R, D), f32),
            V((F, NB, BLOCK), f32), V((F, NB, BLOCK), f32),
            V((ITERS, 2, 128), f32), V((ITERS, N, 2, 128), f32),
            V((F, NB, BLOCK), f32), V((1, D), f32),
            dma((F, CH)), dma((5,)), dma((2,)), dma((3,)), dma((2,)), dma((2,)), dma((ITERS, 2)), dma((2,)),
        ],
        compiler_params=pltpu.CompilerParams(
            collective_id=0, has_side_effects=True, vmem_limit_bytes=63 * 1024 * 1024),
    )(photons, jnp.transpose(masses, (1, 2, 0)), maps, model.reshape(MB, BLOCK),
      fluence.reshape(1, D), level_scale.reshape(1, L))
    return gain.reshape(-1), phi.reshape(-1)


def solution(mesh):
    placed = (
        P(("grp", "frame"), "orient"),
        P(("grp", "frame"), "orient", None),
        P("orient", None),
        P("grp"),
        P(("grp", "frame")),
        P(),
    )
    O, F = mesh.shape["orient"], mesh.shape["frame"]

    def run(*args):
        return on_device(O, F, *args)

    return jax.shard_map(
        run,
        mesh=mesh,
        in_specs=placed,
        out_specs=(P(("grp", "orient")), P(("grp", "frame"))),
        check_vma=False,
    )
```
